128 devices in a mesh: segment: 4 (over z_lo, core), tile: 32 (over y, x, z_hi).
Axes of the slice: x: 4, y: 4, z: 4 (z_hi: 2, z_lo: 2; z = z_hi * 2 + z_lo), core: 2. Of those that a mesh axis runs over, the one named last changes fastest.
Arguments:
- fields: bfloat16 [4, 4, 6, 384, 384], P(None, None, None, 'tile'), may hold values from -6 to 6
- valid_mask: int32 [6, 384, 64], P(None, 'tile'), may hold values 0 or 1
- targets: float32 [4, 6, 384, 256], P(None, None, 'tile'), may hold values from -8 to 17
- w_embed: bfloat16 [384, 512], replicated, may hold values from -0.3125 to 0.3125
- level_embed: bfloat16 [4, 512], replicated, may hold values from -6 to 6
- lat_query: bfloat16 [4, 512], replicated, may hold values from -6 to 6
- w_query: bfloat16 [512, 512], replicated, may hold values from -0.25 to 0.25
- w_key: bfloat16 [512, 512], replicated, may hold values from -0.25 to 0.25
- w_value: bfloat16 [512, 512], replicated, may hold values from -0.25 to 0.25
- w_enc_out: bfloat16 [512, 512], replicated, may hold values from -0.25 to 0.25
- gain_attn: bfloat16 [4, 512], P('segment'), may hold values from 0.5 to 1.5
- w_qkv: bfloat16 [4, 512, 1536], P('segment'), may hold values from -0.25 to 0.25
- w_proj: bfloat16 [4, 512, 512], P('segment'), may hold values from -0.25 to 0.25
- gain_mlp: bfloat16 [4, 512], P('segment'), may hold values from 0.5 to 1.5
- w_up: bfloat16 [4, 512, 2048], P('segment'), may hold values from -0.25 to 0.25
- w_down: bfloat16 [4, 2048, 512], P('segment'), may hold values from -0.125 to 0.125
- gain_dec: bfloat16 [512], replicated, may hold values from 0.5 to 1.5
- w_dec: bfloat16 [4, 512, 256], replicated, may hold values from -0.125 to 0.125
- shifts: int32 [4], P('segment'), may hold values from 1 to 11
Outputs:
- predictions: bfloat16 [4, 6, 384, 256], P('segment', None, 'tile')
- nse_score: float32 [4], replicated
- kge_score: float32 [4], replicated
The draws below stay inside these ranges and needn't reach their ends.
All inputs are finite; a program needn't handle non-finite values. No bound on the sum of `valid_mask` on one device may be relied on, other than what follows from the above.
Results may differ from the reference program's by a relative error of at most 0.025.
Values may be sent and summed in bfloat16 or wider, within the bound.
No kernel may reach another device: no remote copies, remote signals or barrier semaphores. Data moves between devices by JAX's collectives and lax.ppermute only.
A program may use at most 128 MiB of HBM per device.

```python
import math
import jax
import jax.numpy as jnp
from jax import lax

D = 512
HEADS = 16
FF = 2048
LATL = 4
LEV_IN = 4
HV = 4
WLEV = 2
WLAT = 6
WLON = 12
LAT = 6
PP = 64
FEAT = 384
HVF = 256
SEGMENTS = 4
M = 4
LONG = 384


def draw_targets(key, part):
    key = jax.random.fold_in(key, 11)
    level_key, spread_key, noise_key = jax.random.split(key, 3)
    level = jax.random.uniform(level_key, (HV,), jnp.float32, 1.0, 3.0)
    spread = jnp.exp(jax.random.uniform(spread_key, (HV,), jnp.float32, math.log(0.3), math.log(2.0)))
    level_full = jnp.repeat(level, PP)
    spread_full = jnp.repeat(spread, PP)
    shape = (M, LAT, LONG, HVF)
    noise = jnp.clip(jax.random.normal(noise_key, shape, jnp.float32), -4.0, 4.0)
    ramp = 1.0 + 2.0 * jnp.arange(LONG, dtype=jnp.float32).reshape(1, 1, LONG, 1) / LONG
    return level_full * ramp + spread_full * noise


def set_ends(values, rng, least, largest):
    place = [jax.random.randint(jax.random.fold_in(rng, axis), (), 0, length) for axis, length in enumerate(values.shape)]
    widest = values.shape.index(max(values.shape))
    beside = place[:widest] + [(place[widest] + 1) % values.shape[widest]] + place[widest + 1:]
    return values.at[tuple(place)].set(least).at[tuple(beside)].set(largest)


def block_levels(own_key, extent, cuts, least, top_value):
    gain, own = 1.0, jax.random.fold_in(own_key, 6)
    for position, blocks in cuts:
        steps = jnp.exp(jax.random.uniform(jax.random.fold_in(own, position), (blocks,), jnp.float32, least / len(cuts), top_value / len(cuts)))
        gain = gain * jnp.repeat(steps, extent[position] // blocks).reshape([-1 if axis == position else 1 for axis in range(len(extent))])
    return gain


def gaussian(stream_key, extent, scale, limit, shards=(), held_as=jnp.bfloat16):
    gain = block_levels(stream_key, extent, shards, -0.22, 0.18) if shards else 1.0
    array = jax.random.normal(stream_key, extent, jnp.float32) * scale * gain
    return jnp.minimum(jnp.maximum(array, -limit), limit).astype(held_as)


def setup_inputs(seed: int = 0) -> dict:
    keys = jax.random.split(jax.random.key(seed), 20)
    fields = gaussian(keys[0], (M, LEV_IN, LAT, LONG, FEAT), 1.0, 6.0, ((3, 32),))
    valid_mask = set_ends((jax.random.randint(keys[1], (LAT, LONG, PP), 0, 4) < 3).astype(jnp.int32), jax.random.fold_in(keys[1], 1), 0, 1)
    targets = draw_targets(jax.random.fold_in(keys[19], 71), 0)
    w_embed = gaussian(keys[3], (FEAT, D), FEAT ** -0.5, 0.3125)
    level_embed = gaussian(keys[4], (LEV_IN, D), 1.0, 6.0)
    lat_query = gaussian(keys[5], (LATL, D), 1.0, 6.0)
    w_query = gaussian(keys[6], (D, D), D ** -0.5, 0.25)
    w_key = gaussian(keys[7], (D, D), D ** -0.5, 0.25)
    w_value = gaussian(keys[8], (D, D), D ** -0.5, 0.25)
    w_enc_out = gaussian(keys[9], (D, D), D ** -0.5, 0.25)
    gain_attn = jnp.clip(1.0 + 0.1 * jax.random.normal(keys[10], (SEGMENTS, D), jnp.float32), 0.5, 1.5).astype(jnp.bfloat16)
    w_qkv = gaussian(keys[11], (SEGMENTS, D, 3 * D), D ** -0.5, 0.25, ((0, 4),))
    w_proj = gaussian(keys[12], (SEGMENTS, D, D), D ** -0.5, 0.25, ((0, 4),))
    gain_mlp = jnp.clip(1.0 + 0.1 * jax.random.normal(keys[13], (SEGMENTS, D), jnp.float32), 0.5, 1.5).astype(jnp.bfloat16)
    w_up = gaussian(keys[14], (SEGMENTS, D, FF), D ** -0.5, 0.25, ((0, 4),))
    w_down = gaussian(keys[15], (SEGMENTS, FF, D), FF ** -0.5, 0.125, ((0, 4),))
    gain_dec = jnp.clip(1.0 + 0.1 * jax.random.normal(keys[16], (D,), jnp.float32), 0.5, 1.5).astype(jnp.bfloat16)
    w_dec = gaussian(keys[17], (LATL, D, HVF), (LATL * D) ** -0.5, 0.125)
    shifts = set_ends(jax.random.randint(keys[18], (SEGMENTS,), 1, WLON), jax.random.fold_in(keys[18], 1), 1, WLON - 1).astype(jnp.int32)
    return dict(fields=fields, valid_mask=valid_mask, targets=targets, w_embed=w_embed, level_embed=level_embed, lat_query=lat_query, w_query=w_query, w_key=w_key, w_value=w_value, w_enc_out=w_enc_out, gain_attn=gain_attn, w_qkv=w_qkv, w_proj=w_proj, gain_mlp=gain_mlp, w_up=w_up, w_down=w_down, gain_dec=gain_dec, w_dec=w_dec, shifts=shifts)


EPSILON = 1e-05

def project(values, weight):
    leading = values.shape[:-1]
    flattened = values.reshape(-1, values.shape[-1])
    result = jnp.dot(flattened, weight, preferred_element_type=jnp.float32)
    return result.reshape(leading + (weight.shape[-1],))

def norm_rows(values, gain_vec):
    values = values.astype(jnp.float32)
    centred = values - lax.optimization_barrier(jnp.mean(values, -1, keepdims=True))
    spread = lax.optimization_barrier(jnp.mean(centred * centred, -1, keepdims=True))
    return centred * lax.rsqrt(spread + EPSILON) * gain_vec.astype(jnp.float32)

def encode(fields, mask_feat, w_embed, level_embed, lat_query, w_query, w_key, w_value, w_enc_out):
    masked = fields * mask_feat
    embedded = (project(masked, w_embed) + level_embed.astype(jnp.float32)[None, :, None, None, :]).astype(jnp.bfloat16)
    key_rows = project(embedded, w_key).astype(jnp.bfloat16)
    value_rows = project(embedded, w_value).astype(jnp.bfloat16)
    queries = project(lat_query, w_query).astype(jnp.bfloat16)
    batches, levels, lat_rows, columns, features = key_rows.shape
    headsize = features // HEADS
    key_rows = key_rows.reshape(batches, levels, lat_rows, columns, HEADS, headsize).astype(jnp.float32)
    value_rows = value_rows.reshape(batches, levels, lat_rows, columns, HEADS, headsize).astype(jnp.float32)
    latents = queries.shape[0]
    queries = queries.reshape(latents, HEADS, headsize).astype(jnp.float32)
    scores = jnp.einsum('qhe,blrche->brchql', queries, key_rows) * headsize ** (-0.5)
    weights = jax.nn.softmax(scores, axis=-1).astype(jnp.bfloat16)
    mixture = jnp.einsum('brchql,blrche->bqrche', weights.astype(jnp.float32), value_rows).astype(jnp.bfloat16)
    mixture = mixture.reshape(batches, latents, lat_rows, columns, features)
    return project(mixture, w_enc_out).astype(jnp.bfloat16)

def attend(tokens, gain_vec, qkv_weight):
    levels, lat_rows, columns, features = tokens.shape
    headsize = features // HEADS
    normed = norm_rows(tokens, gain_vec).astype(jnp.bfloat16)
    packed = project(normed, qkv_weight).astype(jnp.bfloat16)
    shaped = packed.reshape(levels // WLEV, WLEV, lat_rows // WLAT, WLAT, columns // WLON, WLON, 3, HEADS, headsize)
    shaped = shaped.transpose(6, 0, 2, 4, 7, 1, 3, 5, 8).reshape(3, -1, HEADS, WLEV * WLAT * WLON, headsize)
    queries = shaped[0].astype(jnp.float32)
    key_rows = shaped[1].astype(jnp.float32)
    value_rows = shaped[2].astype(jnp.float32)
    scores = jnp.einsum('nhte,nhse->nhts', queries, key_rows) * headsize ** (-0.5)
    weights = jax.nn.softmax(scores, axis=-1).astype(jnp.bfloat16)
    mixture = jnp.einsum('nhts,nhse->nhte', weights.astype(jnp.float32), value_rows).astype(jnp.bfloat16)
    mixture = mixture.reshape(levels // WLEV, lat_rows // WLAT, columns // WLON, HEADS, WLEV, WLAT, WLON, headsize)
    return mixture.transpose(0, 4, 1, 5, 2, 6, 3, 7).reshape(levels, lat_rows, columns, features)

def finish(tokens, mixture, proj_weight, gain_vec, up_weight, down_weight):
    resid = tokens.astype(jnp.float32) + project(mixture, proj_weight)
    normed = norm_rows(resid, gain_vec).astype(jnp.bfloat16)
    hidden = jax.nn.gelu(project(normed, up_weight)).astype(jnp.bfloat16)
    return (resid + project(hidden, down_weight)).astype(jnp.bfloat16)

def decode(current, gain_dec, w_dec):
    normed = norm_rows(current, gain_dec).astype(jnp.bfloat16)
    summed = project(normed[0], w_dec[0])
    for level in range(1, normed.shape[0]):
        summed = summed + project(normed[level], w_dec[level])
    return summed

def partial_sums(estimate, observed, validity):
    lat_rows, columns, outputs = observed.shape
    pixels = validity.shape[-1]
    shape = (lat_rows, columns, outputs // pixels, pixels)
    guess = estimate.reshape(shape)
    truth = observed.reshape(shape)
    weight = validity[:, :, None, :]
    misfit = guess - truth
    summands = [weight * jnp.ones_like(truth), weight * truth, weight * truth * truth, weight * guess, weight * guess * guess, weight * guess * truth, weight * misfit * misfit]
    return jnp.stack([lax.optimization_barrier(jnp.sum(term, axis=(0, 1, 3))) for term in summands])

def scores_of(totals):
    number = jnp.maximum(totals[0], 1.0)
    mean_obs = totals[1] / number
    var_obs = totals[2] / number - mean_obs * mean_obs
    mean_pred = totals[3] / number
    var_pred = totals[4] / number - mean_pred * mean_pred
    covariance = totals[5] / number - mean_pred * mean_obs
    nse_score = 1.0 - totals[6] / (number * var_obs)
    correlation = covariance / jnp.sqrt(var_pred * var_obs + EPSILON)
    spread_ratio = jnp.sqrt((var_pred + EPSILON) / var_obs)
    mean_ratio = mean_pred / mean_obs
    kge_score = 1.0 - jnp.sqrt((correlation - 1.0) ** 2 + (spread_ratio - 1.0) ** 2 + (mean_ratio - 1.0) ** 2)
    return (nse_score, kge_score)

def reference(fields, valid_mask, targets, w_embed, level_embed, lat_query, w_query, w_key, w_value, w_enc_out, gain_attn, w_qkv, w_proj, gain_mlp, w_up, w_down, gain_dec, w_dec, shifts):
    repeats = fields.shape[-1] // valid_mask.shape[-1]
    mask_feat = jnp.tile(valid_mask.astype(jnp.bfloat16), (1, 1, repeats))
    validity = valid_mask.astype(jnp.float32)
    latent = encode(fields, mask_feat, w_embed, level_embed, lat_query, w_query, w_key, w_value, w_enc_out)
    outputs = []
    summed = jnp.zeros((7, targets.shape[-1] // valid_mask.shape[-1]), jnp.float32)
    for item in range(fields.shape[0]):
        current = latent[item]
        for section_no in range(shifts.shape[0]):
            offset = shifts[section_no]
            rolled = jnp.roll(current, -offset, axis=2)
            mixture = attend(rolled, gain_attn[section_no], w_qkv[section_no])
            section_out = finish(rolled, mixture, w_proj[section_no], gain_mlp[section_no], w_up[section_no], w_down[section_no])
            current = jnp.roll(section_out, offset, axis=2)
        estimate = decode(current, gain_dec, w_dec)
        outputs.append(estimate.astype(jnp.bfloat16))
        summed = summed + partial_sums(estimate, targets[item], validity)
    nse_score, kge_score = scores_of(summed)
    return (jnp.stack(outputs), nse_score, kge_score)
```

```python
import functools

import jax
import jax.numpy as jnp
from jax import lax
from jax.experimental import pallas as pl
from jax.experimental.pallas import tpu as pltpu
from jax.sharding import PartitionSpec as P

HEADS = 16
WLON = 12
EPSILON = 1e-05
PAD = 16
REACH = 2
LOG2E = 1.4426950408889634
SQRT_2_OVER_PI = 0.7978845608028654
WINDOW = 144
F32 = jnp.float32
BF16 = jnp.bfloat16

VMEM = pl.BlockSpec(memory_space=pltpu.VMEM)
SMEM = pl.BlockSpec(memory_space=pltpu.SMEM)
ANY = pl.BlockSpec(memory_space=pl.ANY)


def params(mib, **more):
    return pltpu.CompilerParams(vmem_limit_bytes=mib * 2**20, **more)


def mm(a, b):
    return jnp.dot(a, b, preferred_element_type=F32)


def mm_t(a, b):
    return lax.dot_general(a, b, (((1,), (1,)), ((), ())), preferred_element_type=F32)


def norm(x, gain):
    centred = x - jnp.mean(x, -1, keepdims=True)
    spread = jnp.mean(centred * centred, -1, keepdims=True)
    return centred * lax.rsqrt(spread + EPSILON) * gain.astype(F32)


def masks_and_queries(mask_ref, lat_query, wq, wk, small, mask_out, kq_out, latents, feat):
    lats, cols, cells = mask_ref.shape
    d = wk.shape[0]
    width = d // HEADS
    n_q = latents * HEADS
    for i in range(lats):
        small[i * cols:(i + 1) * cols, :] = mask_ref[i].astype(F32)
    repeat = (
        lax.broadcasted_iota(jnp.int32, (cells, feat), 1) % cells
        == lax.broadcasted_iota(jnp.int32, (cells, feat), 0)
    ).astype(F32).astype(BF16)
    levels = mask_out.shape[0] // small.shape[0]
    expand = (
        lax.broadcasted_iota(jnp.int32, (mask_out.shape[0], small.shape[0]), 0) // levels
        == lax.broadcasted_iota(jnp.int32, (mask_out.shape[0], small.shape[0]), 1)
    ).astype(F32).astype(BF16)
    wide = mm(small[...].astype(BF16), repeat).astype(BF16)
    mask_out[...] = mm(expand, wide).astype(BF16)
    queries = mm(lat_query[...], wq[...]).astype(BF16)
    pick = (
        lax.broadcasted_iota(jnp.int32, (latents, n_q), 1) // HEADS
        == lax.broadcasted_iota(jnp.int32, (latents, n_q), 0)
    ).astype(F32).astype(BF16)
    spread = lax.dot_general(queries, pick, (((0,), (0,)), ((), ())), preferred_element_type=F32)
    own = (
        lax.broadcasted_iota(jnp.int32, (d, n_q), 0) // width
        == lax.broadcasted_iota(jnp.int32, (d, n_q), 1) % HEADS
    )
    kq_out[...] = mm(wk[...], jnp.where(own, spread, 0.0).astype(BF16)).astype(BF16)


def encode_unit(f_ref, score_ref, value_ref, mask, kq, we, le, wv, wo):
    lats, cols, levels, feat = f_ref.shape
    d = we.shape[1]
    rows = lats * cols
    n_q = kq.shape[1]
    latents = n_q // HEADS
    width = d // HEADS
    masked = f_ref[...].astype(F32).reshape(rows * levels, feat).astype(BF16) * mask[...]
    tiled = jnp.concatenate([le[...].astype(F32)] * (8 // levels), 0)
    embedded = mm(masked, we[...]).reshape(rows * levels // 8, 8, d) + tiled[None]
    embedded = embedded.reshape(rows * levels, d).astype(BF16)
    score_ref[:, :n_q] = mm(embedded, kq[...]) * (width ** -0.5)
    values = mm(embedded, wv[...]).astype(BF16).astype(F32)
    strips = d // 128
    for i in range(strips):
        value_ref[i] = values[:, i * 128:(i + 1) * 128]
    parts = [score_ref[pl.ds(l, rows, levels), :][:, :n_q] for l in range(levels)]
    values = [
        jnp.concatenate([value_ref[i, pl.ds(l, rows, levels), :] for i in range(strips)], 1) for l in range(levels)
    ]
    top = parts[0]
    for part in parts[1:]:
        top = jnp.maximum(top, part)
    parts = [jnp.exp(part - top) for part in parts]
    total = parts[0]
    for part in parts[1:]:
        total = total + part
    probs = jnp.concatenate([part / total for part in parts], 0).astype(BF16)
    mixed = []
    for q in range(latents):
        widen = (
            lax.broadcasted_iota(jnp.int32, (n_q, d), 0)
            == lax.broadcasted_iota(jnp.int32, (n_q, d), 1) // width + q * HEADS
        ).astype(F32).astype(BF16)
        wide = mm(probs, widen)
        acc = wide[:rows] * values[0]
        for l in range(1, levels):
            acc = acc + wide[l * rows:(l + 1) * rows] * values[l]
        mixed.append(acc)
    return mm(jnp.concatenate(mixed, 0).astype(BF16), wo[...]).astype(BF16)


def start_kernel(n_big, *refs):
    fields, mask_ref, lat_query, wq, wk, *rest = refs
    big, rest = rest[:n_big], rest[n_big:]
    o_ref, mask_out, kq_out = rest[:3]
    held, rest = rest[3:3 + n_big], rest[3 + n_big:]
    f_buf, wq_buf, wk_buf, mask_buf, score_ref, value_ref, small, sems, more = rest
    we, le, wv, wo = held[:4]
    early = [
        pltpu.make_async_copy(s, t, more.at[i])
        for i, (s, t) in enumerate([(mask_ref, mask_buf), (wq, wq_buf), (wk, wk_buf), (fields.at[lax.axis_index("segment") % 2], f_buf)])
    ]
    copies = [pltpu.make_async_copy(s, t, sems.at[i]) for i, (s, t) in enumerate(zip(big, held))]
    for c in early + copies:
        c.start()
    for c in early + copies[:4]:
        c.wait()
    n = o_ref.shape[0] - PAD
    latents = lat_query.shape[0]
    masks_and_queries(mask_buf, lat_query, wq_buf, wk_buf, small, mask_out, kq_out, latents, f_buf.shape[-1])
    o_ref[:n, :] = encode_unit(f_buf, score_ref, value_ref, mask_out, kq_out, we, le, wv, wo)
    o_ref[n:, :] = jnp.zeros((PAD, o_ref.shape[1]), BF16)
    for c in copies[4:]:
        c.wait()


def start(fields, valid_mask, lat_query, w_query, w_key, big):
    _, lats, cols, levels, feat = fields.shape
    latents, d = lat_query.shape
    cells = valid_mask.shape[-1]
    rows = lats * cols
    n = latents * rows
    hbm = [pltpu.with_memory_space_constraint(a, pltpu.HBM) for a in (fields, valid_mask)]
    more = [pltpu.with_memory_space_constraint(a, pltpu.HBM) for a in (w_query, w_key, *big)]
    out = pl.pallas_call(
        lambda *refs: start_kernel(len(big), *refs),
        in_specs=[ANY, ANY, VMEM] + [ANY] * (2 + len(big)),
        out_specs=[VMEM] * (3 + len(big)),
        out_shape=[
            jax.ShapeDtypeStruct((n + PAD, d), BF16),
            pltpu.VMEM((rows * levels, feat), BF16),
            pltpu.VMEM((d, latents * HEADS), BF16),
        ] + [pltpu.VMEM(a.shape, a.dtype) for a in big],
        scratch_shapes=[
            pltpu.VMEM(fields.shape[1:], BF16),
            pltpu.VMEM(w_query.shape, BF16),
            pltpu.VMEM(w_key.shape, BF16),
            pltpu.VMEM(valid_mask.shape, jnp.int32),
            pltpu.VMEM((rows * levels, 128), F32),
            pltpu.VMEM((d // 128, rows * levels, 128), F32),
            pltpu.VMEM((rows, cells), F32),
            pltpu.SemaphoreType.DMA((len(big),)),
            pltpu.SemaphoreType.DMA((4,)),
        ],
        compiler_params=params(24),
        cost_estimate=pl.CostEstimate(flops=10**9, bytes_accessed=10**7, transcendentals=0),
        name="start",
    )(*hbm, lat_query, *more)
    return out[0], out[1:3], out[3:]


def own_slots(slot, before, after, rightward):
    held = (slot < before).astype(jnp.int32)
    wanted = (slot < after).astype(jnp.int32)
    wrapped = (after < before).astype(jnp.int32) if rightward else -(after > before).astype(jnp.int32)
    return wanted + wrapped == held


def gelu(x):
    cubic = SQRT_2_OVER_PI * 0.044715
    t = jnp.tanh(x * (x * x * jnp.asarray(cubic, x.dtype) + jnp.asarray(SQRT_2_OVER_PI, x.dtype)))
    half = x * jnp.asarray(0.5, x.dtype)
    return half * t + half


def attend(qkv_ref, mix_ref, lanes, d, width):
    window = qkv_ref.shape[0]
    per = lanes // width
    head_of = lax.broadcasted_iota(jnp.int32, (window, lanes), 1) // width
    row = lax.broadcasted_iota(jnp.int32, (1, lanes), 1) // width
    only = [(row == h).astype(F32).astype(BF16) for h in range(per)]
    ones = jnp.ones((window, lanes), BF16)
    for lo in range(0, d, lanes):
        q = qkv_ref[:, lo:lo + lanes]
        k = qkv_ref[:, d + lo:d + lo + lanes]
        v = qkv_ref[:, 2 * d + lo:2 * d + lo + lanes]
        scores = mm_t(jnp.concatenate([q * mask for mask in only], 0), k)
        probs = jnp.exp2((scores - jnp.max(scores, -1, keepdims=True)).astype(BF16))
        both = mm(probs, jnp.concatenate([v, ones], 1))
        num = both[:window, :lanes]
        den = both[:window, lanes:]
        for h in range(1, per):
            mine = head_of == h
            num = jnp.where(mine, both[h * window:(h + 1) * window, :lanes], num)
            den = jnp.where(mine, both[h * window:(h + 1) * window, lanes:], den)
        mix_ref[:, lo:lo + lanes] = (num / den).astype(BF16)
    return mix_ref[...]


def run_section(index, own_ref, nbr_ref, small, wqkv, wproj, wup, wdown, o_ref, qkv_ref, mix_ref):
    n, d = o_ref.shape[0] - PAD, o_ref.shape[1]
    width = d // HEADS
    window = qkv_ref.shape[0]
    passed = own_ref[n:, :].astype(F32)
    place = lax.broadcasted_iota(jnp.int32, (PAD, d), 0)
    shift = small[2:3, :].astype(F32)
    o_ref[n:, :] = jnp.where(place == index, shift, passed).astype(BF16)
    shift = shift[:, :1].astype(jnp.int32)
    before = jnp.sum(jnp.where(place == index - 1, passed, 0.0), 0, keepdims=True)[:, :1].astype(jnp.int32)
    slot = lax.broadcasted_iota(jnp.int32, (window, 1), 0) % WLON
    own = own_slots(slot, before, shift, index % 2 == 0)
    scale = width ** -0.5 * LOG2E

    @pl.loop(0, n // window)
    def _(w):
        at = pl.ds(pl.multiple_of(w * window, window), window)
        rolled = jnp.where(own, own_ref[at, :].astype(F32), nbr_ref[at, :].astype(F32))
        normed = norm(rolled, small[0:1, :]).astype(BF16)
        qkv_ref[:, :d] = (mm(normed, wqkv[0, :, :d]) * scale).astype(BF16)
        qkv_ref[:, d:] = mm(normed, wqkv[0, :, d:]).astype(BF16)
        acc = rolled + mm(attend(qkv_ref, mix_ref, 128, d, width), wproj[0])
        normed = norm(acc, small[1:2, :]).astype(BF16)
        step = 512
        for j in range(0, wup.shape[-1], step):
            hidden = gelu(mm(normed, wup[0, :, j:j + step]).astype(BF16))
            acc = acc + mm(hidden, wdown[0, j:j + step, :])
        o_ref[at, :] = acc.astype(BF16)


def tick_kernel(base, turn, own_ref, nbr_ref, *refs):
    given, received = refs[:5], refs[5:10]
    rest = refs[10:]
    mine = lax.axis_index("segment") % 2 == turn

    @pl.when(mine)
    def _():
        run_section(base + turn, own_ref, nbr_ref, *given, *rest)

    @pl.when(jnp.logical_not(mine))
    def _():
        run_section(base + turn, own_ref, nbr_ref, *received, *rest)


def tick(base, turn, own, nbr, given, received):
    rows, d = own.shape
    return pl.pallas_call(
        functools.partial(tick_kernel, base, turn),
        in_specs=[VMEM] * 12,
        out_specs=VMEM,
        out_shape=jax.ShapeDtypeStruct((rows, d), BF16),
        scratch_shapes=[pltpu.VMEM((WINDOW, 3 * d), BF16), pltpu.VMEM((WINDOW, d), BF16)],
        compiler_params=params(24),
        cost_estimate=pl.CostEstimate(flops=8 * 10**9, bytes_accessed=8 * 10**6, transcendentals=0),
        name="section",
    )(own, nbr, *given, *received)


def decode_kernel(state_ref, gain, w_ref, *refs):
    *arrived, o_ref = refs[:-1] if len(refs) == 3 else refs
    latents = w_ref.shape[0]
    n = state_ref.shape[0] - PAD
    rows = n // latents
    ours = lax.axis_index("segment") // 2 == 1

    @pl.when(ours)
    def _():
        normed = norm(state_ref[:n, :].astype(F32), gain[...])
        total = mm(normed[:rows].astype(BF16), w_ref[0])
        for i in range(1, latents):
            total = total + mm(normed[i * rows:(i + 1) * rows].astype(BF16), w_ref[i])
        passed = state_ref[n:, :o_ref.shape[1]].astype(F32)[:8]
        o_ref[...] = jnp.concatenate([total, passed], 0).astype(BF16)

    if arrived:
        @pl.when(jnp.logical_not(ours))
        def _():
            o_ref[...] = arrived[0][...]

        s = o_ref[...].astype(F32)[rows:]
        s = [s[i:i + 1, :] for i in range(4)]
        turns = jnp.zeros_like(s[0])
        for i in range(1, 4):
            if i % 2 == 0:
                turns = turns + (s[i] < s[i - 1]).astype(F32)
            else:
                turns = turns - (s[i] > s[i - 1]).astype(F32)
        refs[-1][0] = jnp.max(turns).astype(jnp.int32) + REACH


def decode(state, gain_dec, w_dec, *arrived):
    latents, _, outputs = w_dec.shape
    rows = (state.shape[0] - PAD) // latents
    more = len(arrived)
    return pl.pallas_call(
        decode_kernel,
        in_specs=[VMEM] * (3 + more),
        out_specs=[VMEM] + [SMEM] * more,
        out_shape=[jax.ShapeDtypeStruct((rows + 8, outputs), BF16)] + [jax.ShapeDtypeStruct((1,), jnp.int32)] * more,
        compiler_params=params(24),
        cost_estimate=pl.CostEstimate(flops=10**9, bytes_accessed=10**6, transcendentals=0),
        name="decode",
    )(state, gain_dec, w_dec, *arrived)


def home_kernel(*refs):
    same, before, mask_ref, targets, o_ref, sums_ref, x_ref, t_buf, t_ref, sem = refs
    copy = pltpu.make_async_copy(targets.at[:, :, lax.axis_index("segment")], t_buf, sem)
    copy.start()
    _, lats, cols, outs = o_ref.shape
    rows = lats * cols
    cells = mask_ref.shape[-1]
    shift = same[rows:, :].astype(F32)[3:4, :1].astype(jnp.int32)
    slot = lax.broadcasted_iota(jnp.int32, (rows, 1), 0) % WLON
    repeat = (
        lax.broadcasted_iota(jnp.int32, (cells, outs), 1) % cells
        == lax.broadcasted_iota(jnp.int32, (cells, outs), 0)
    ).astype(F32).astype(BF16)
    for i in range(lats):
        x_ref[i * cols:(i + 1) * cols, :cells] = mask_ref[i].astype(F32)
    weight = mm(x_ref[:, :cells].astype(BF16), repeat)
    guess = jnp.where(slot < shift, before[:rows, :].astype(F32), same[:rows, :].astype(F32))
    x_ref[...] = guess
    for i in range(lats):
        o_ref[0, i] = x_ref[i * cols:(i + 1) * cols, :].astype(BF16)
    copy.wait()
    for i in range(lats):
        x_ref[i * cols:(i + 1) * cols, :] = t_buf[i]
    truth = x_ref[...]
    misfit = guess - truth
    terms = (
        weight, weight * truth, weight * truth * truth, weight * guess, weight * guess * guess,
        weight * guess * truth, weight * misfit * misfit,
    )
    t_ref[...] = jnp.zeros(t_ref.shape, F32)
    for i, term in enumerate(terms):
        t_ref[i:i + 1, :] = jnp.sum(term, 0, keepdims=True)
    table = t_ref[...]
    n_var = outs // cells
    var_of = lax.broadcasted_iota(jnp.int32, table.shape, 1) // cells
    shape = (8, sums_ref.shape[-1])
    lane = lax.broadcasted_iota(jnp.int32, shape, 1)
    row = lax.broadcasted_iota(jnp.int32, shape, 0)
    flat = jnp.zeros(shape, F32)
    for v in range(n_var):
        part = jnp.sum(jnp.where(var_of == v, table, 0.0), -1, keepdims=True)
        flat = jnp.where(lane == row * n_var + v, part, flat)
    sums_ref[...] = jnp.broadcast_to(jnp.sum(flat, 0, keepdims=True), sums_ref.shape)


def at_home(cands, valid_mask, targets, devices):
    lats, cols, _, outs = targets.shape
    return pl.pallas_call(
        home_kernel,
        in_specs=[VMEM] * (len(cands) + 1) + [ANY],
        out_specs=[VMEM, VMEM],
        out_shape=[
            jax.ShapeDtypeStruct((1, lats, cols, outs), BF16),
            jax.ShapeDtypeStruct((devices, 128), F32),
        ],
        scratch_shapes=[
            pltpu.VMEM((lats * cols, outs), F32), pltpu.VMEM((lats, cols, outs), F32),
            pltpu.VMEM((8, outs), F32), pltpu.SemaphoreType.DMA,
        ],
        compiler_params=params(32),
        cost_estimate=pl.CostEstimate(flops=10**8, bytes_accessed=10**6, transcendentals=0),
        name="home",
    )(*cands, valid_mask, pltpu.with_memory_space_constraint(targets, pltpu.HBM))


def score_kernel(sums_ref, nse_ref, kge_ref, t_ref):
    n_var = nse_ref.shape[-1]
    total = jnp.sum(sums_ref[...], 0, keepdims=True)
    t_ref[...] = jnp.broadcast_to(total, t_ref.shape)
    t = [t_ref[:1, i * n_var:(i + 1) * n_var] for i in range(7)]
    number = jnp.maximum(t[0], 1.0)
    mean_obs = t[1] / number
    var_obs = t[2] / number - mean_obs * mean_obs
    mean_pred = t[3] / number
    var_pred = t[4] / number - mean_pred * mean_pred
    covariance = t[5] / number - mean_pred * mean_obs
    nse_ref[...] = 1.0 - t[6] / (number * var_obs)
    correlation = covariance / jnp.sqrt(var_pred * var_obs + EPSILON)
    spread_ratio = jnp.sqrt((var_pred + EPSILON) / var_obs)
    mean_ratio = mean_pred / mean_obs
    kge_ref[...] = 1.0 - jnp.sqrt(
        (correlation - 1.0) ** 2 + (spread_ratio - 1.0) ** 2 + (mean_ratio - 1.0) ** 2
    )


def scores(sums, n_var):
    return pl.pallas_call(
        score_kernel,
        in_specs=[VMEM],
        out_specs=[VMEM, VMEM],
        out_shape=[jax.ShapeDtypeStruct((1, n_var), F32)] * 2,
        scratch_shapes=[pltpu.VMEM((8, sums.shape[-1]), F32)],
        name="scores",
    )(sums)


def along(x, axis, distance):
    size = lax.axis_size(axis)
    return lax.ppermute(x, axis, [(i, (i + distance) % size) for i in range(size)])


def to_next_stage(x, turned):
    sections, tiles = lax.axis_size("segment"), lax.axis_size("tile")
    step = -1 if turned else 0
    route = [
        (k * tiles + t, (k + 2) % sections * tiles + (t + step) % tiles) for k in range(sections) for t in range(tiles)
    ]
    return lax.ppermute(x, ("segment", "tile"), route)


def from_other_core(x):
    return lax.ppermute(x, "segment", [(k, k ^ 1) for k in range(lax.axis_size("segment"))])


def way_home(turns, pred):
    return [pred if step == 0 else along(pred, "tile", step) for step in (turns, turns + 1)]


def local(
    fields, valid_mask, targets, w_embed, level_embed, lat_query, w_query, w_key, w_value, w_enc_out,
    gain_attn, w_qkv, w_proj, gain_mlp, w_up, w_down, gain_dec, w_dec, shifts,
):
    sections, tiles = lax.axis_size("segment"), lax.axis_size("tile")
    d = gain_attn.shape[1]
    shift_row = jnp.broadcast_to(shifts.astype(BF16)[:, None], (1, d))
    given = (jnp.concatenate([gain_attn, gain_mlp, shift_row]), w_qkv, w_proj, w_up, w_down)
    received = [from_other_core(a) for a in given]

    big = (w_embed, level_embed, w_value, w_enc_out, *given, w_dec)
    fields = fields.transpose(0, 2, 3, 1, 4)
    targets = targets.transpose(1, 2, 0, 3)
    latent, (mask, kq), held = start(fields, valid_mask, lat_query, w_query, w_key, big)
    enc = (mask, kq, *held[:4])
    given = held[4:9]
    w_dec = held[9]
    gain_dec = gain_dec[None, :]

    states = [latent]
    nbrs = [along(latent, "tile", -1)]
    states.append(encode(fields, enc))
    nbrs.append(along(states[1], "tile", -1))
    for u in range(2):
        states[u] = tick(0, 0, states[u], nbrs[u], given, received)
        nbrs[u] = along(states[u], "tile", 1)
    for u in range(2):
        state = tick(0, 1, states[u], nbrs[u], given, received)
        states[u], nbrs[u] = to_next_stage(state, False), to_next_stage(state, True)
    for u in range(2):
        states[u] = tick(2, 0, states[u], nbrs[u], given, received)
        nbrs[u] = along(states[u], "tile", 1)
    for u in range(2):
        states[u] = tick(2, 1, states[u], nbrs[u], given, received)
        if u == 0:
            arrived = to_next_stage(decode(states[0], gain_dec, w_dec)[0], False)
    pred, turns = decode(states[1], gain_dec, w_dec, arrived)
    cands = lax.switch(turns[0], [functools.partial(way_home, t - REACH) for t in range(2 * REACH)], pred)
    predictions, sums = at_home(cands, valid_mask, targets, sections * tiles)
    sums = lax.all_to_all(sums, ("segment", "tile"), 0, 0, tiled=True)
    nse, kge = scores(sums, targets.shape[-1] // valid_mask.shape[-1])
    return predictions, nse[0], kge[0]


def encode_kernel(fields, mask, kq, we, le, wv, wo, o_ref, f_buf, score_ref, value_ref, sem):
    copy = pltpu.make_async_copy(fields.at[lax.axis_index("segment") % 2 + 2], f_buf, sem)
    copy.start()
    copy.wait()
    n = o_ref.shape[0] - PAD
    o_ref[:n, :] = encode_unit(f_buf, score_ref, value_ref, mask, kq, we, le, wv, wo)
    o_ref[n:, :] = jnp.zeros((PAD, o_ref.shape[1]), BF16)


def encode(fields, enc):
    _, lats, cols, levels, feat = fields.shape
    d, n_q = enc[1].shape
    n = n_q // HEADS * lats * cols
    return pl.pallas_call(
        encode_kernel,
        in_specs=[ANY] + [VMEM] * len(enc),
        out_specs=VMEM,
        out_shape=jax.ShapeDtypeStruct((n + PAD, d), BF16),
        scratch_shapes=[
            pltpu.VMEM(fields.shape[1:], BF16), pltpu.VMEM((levels * lats * cols, 128), F32),
            pltpu.VMEM((d // 128, levels * lats * cols, 128), F32),
            pltpu.SemaphoreType.DMA,
        ],
        compiler_params=params(24),
        cost_estimate=pl.CostEstimate(flops=10**9, bytes_accessed=10**6, transcendentals=0),
        name="encode",
    )(pltpu.with_memory_space_constraint(fields, pltpu.HBM), *enc)


def solution(mesh):
    placed = (
        P(None, None, None, "tile", None),
        P(None, "tile", None),
        P(None, None, "tile", None),
        P(),
        P(),
        P(),
        P(),
        P(),
        P(),
        P(),
        P("segment", None),
        P("segment", None, None),
        P("segment", None, None),
        P("segment", None),
        P("segment", None, None),
        P("segment", None, None),
        P(),
        P(),
        P("segment"),
    )
    return jax.shard_map(
        local,
        mesh=mesh,
        in_specs=placed,
        out_specs=(P("segment", None, "tile", None), P(), P()),
        check_vma=False,
    )
```

```python
import functools

import jax
import jax.numpy as jnp
from jax import lax
from jax.experimental import pallas as pl
from jax.experimental.pallas import tpu as pltpu
from jax.sharding import PartitionSpec as P

HEADS = 16
WLON = 12
EPSILON = 1e-05
PAD = 16
REACH = 2
LOG2E = 1.4426950408889634
SQRT_2_OVER_PI = 0.7978845608028654
WINDOW = 144
F32 = jnp.float32
BF16 = jnp.bfloat16

VMEM = pl.BlockSpec(memory_space=pltpu.VMEM)
SMEM = pl.BlockSpec(memory_space=pltpu.SMEM)
ANY = pl.BlockSpec(memory_space=pl.ANY)


def params(mib, **more):
    return pltpu.CompilerParams(vmem_limit_bytes=mib * 2**20, **more)


def mm(a, b):
    return jnp.dot(a, b, preferred_element_type=F32)


def mm_t(a, b):
    return lax.dot_general(a, b, (((1,), (1,)), ((), ())), preferred_element_type=F32)


def norm(x, gain):
    centred = x - jnp.mean(x, -1, keepdims=True)
    spread = jnp.mean(centred * centred, -1, keepdims=True)
    return centred * lax.rsqrt(spread + EPSILON) * gain.astype(F32)


def feature_mask(cells_mask, levels, feat):
    rows, cells = cells_mask.shape
    repeat = (
        lax.broadcasted_iota(jnp.int32, (cells, feat), 1) % cells
        == lax.broadcasted_iota(jnp.int32, (cells, feat), 0)
    ).astype(F32).astype(BF16)
    expand = (
        lax.broadcasted_iota(jnp.int32, (rows * levels, rows), 0) // levels
        == lax.broadcasted_iota(jnp.int32, (rows * levels, rows), 1)
    ).astype(F32).astype(BF16)
    return mm(mm(expand, cells_mask.astype(BF16)).astype(BF16), repeat).astype(BF16)


def rows_of(mask_ref, small):
    lats, cols, _ = mask_ref.shape
    for i in range(lats):
        small[i * cols:(i + 1) * cols, :] = mask_ref[i].astype(F32)
    return small[...]


def queries_through_keys(lat_query, wq, wk):
    latents, d = lat_query.shape
    width = d // HEADS
    n_q = latents * HEADS
    queries = mm(lat_query[...], wq[...]).astype(BF16)
    pick = (
        lax.broadcasted_iota(jnp.int32, (latents, n_q), 1) // HEADS
        == lax.broadcasted_iota(jnp.int32, (latents, n_q), 0)
    ).astype(F32).astype(BF16)
    spread = lax.dot_general(queries, pick, (((0,), (0,)), ((), ())), preferred_element_type=F32)
    own = (
        lax.broadcasted_iota(jnp.int32, (d, n_q), 0) // width
        == lax.broadcasted_iota(jnp.int32, (d, n_q), 1) % HEADS
    )
    return mm(wk[...], jnp.where(own, spread, 0.0).astype(BF16)).astype(BF16)


def plus_kernel(w_ref, first_gain, second_gain, shift, o_ref, small_ref):
    d = w_ref.shape[0]
    o_ref[:d, :] = w_ref[...]
    row = lax.broadcasted_iota(jnp.int32, (PAD, d), 0)
    small = jnp.where(row == 0, first_gain[...].astype(F32), second_gain[...].astype(F32))
    small = jnp.where(row < 2, small, shift[0].astype(F32)).astype(BF16)
    o_ref[d:, :] = small
    small_ref[...] = small[:small_ref.shape[0]]


def with_small(weight, first_gain, second_gain, shift):
    rows, d = weight.shape
    return pl.pallas_call(
        plus_kernel,
        in_specs=[VMEM, VMEM, VMEM, SMEM],
        out_specs=[VMEM, VMEM],
        out_shape=[jax.ShapeDtypeStruct((rows + PAD, d), BF16), jax.ShapeDtypeStruct((3, d), BF16)],
        name="plus",
    )(*[pltpu.with_memory_space_constraint(a, pltpu.HBM) for a in (weight, first_gain, second_gain)], shift)


def flat(f_ref):
    lats, cols, levels, feat = f_ref.shape
    return f_ref[...].astype(F32).reshape(lats * cols * levels, feat)


def encode_unit(masked, score_ref, value_ref, kq, we, le, wv, wo):
    d = we.shape[1]
    levels = le.shape[0]
    rows = masked.shape[0] // levels
    n_q = kq.shape[1]
    latents = n_q // HEADS
    width = d // HEADS
    tiled = jnp.concatenate([le[...].astype(F32)] * (8 // levels), 0)
    embedded = mm(masked, we[...]).reshape(rows * levels // 8, 8, d) + tiled[None]
    embedded = embedded.reshape(rows * levels, d).astype(BF16)
    score_ref[:, :n_q] = mm(embedded, kq[...]) * (width ** -0.5)
    values = mm(embedded, wv[...]).astype(BF16).astype(F32)
    strips = d // 128
    for i in range(strips):
        value_ref[i] = values[:, i * 128:(i + 1) * 128]
    parts = [score_ref[pl.ds(l, rows, levels), :][:, :n_q] for l in range(levels)]
    values = [
        jnp.concatenate([value_ref[i, pl.ds(l, rows, levels), :] for i in range(strips)], 1) for l in range(levels)
    ]
    top = parts[0]
    for part in parts[1:]:
        top = jnp.maximum(top, part)
    parts = [jnp.exp(part - top) for part in parts]
    total = parts[0]
    for part in parts[1:]:
        total = total + part
    probs = jnp.concatenate([part / total for part in parts], 0).astype(BF16)
    mixed = []
    for q in range(latents):
        widen = (
            lax.broadcasted_iota(jnp.int32, (n_q, d), 0)
            == lax.broadcasted_iota(jnp.int32, (n_q, d), 1) // width + q * HEADS
        ).astype(F32).astype(BF16)
        wide = mm(probs, widen)
        acc = wide[:rows] * values[0]
        for l in range(1, levels):
            acc = acc + wide[l * rows:(l + 1) * rows] * values[l]
        mixed.append(acc)
    return mm(jnp.concatenate(mixed, 0).astype(BF16), wo[...]).astype(BF16)


def start_kernel(n_big, *refs):
    fields, mask_ref, lat_query, wq, wk, *rest = refs
    big, rest = rest[:n_big], rest[n_big:]
    o_ref, kq_out = rest[:2]
    held, rest = rest[2:2 + n_big], rest[2 + n_big:]
    f_buf, wq_buf, wk_buf, mask_buf, score_ref, value_ref, small, sems, more = rest
    we, le, wv, wo = held[:4]
    early = [
        pltpu.make_async_copy(s, t, more.at[i])
        for i, (s, t) in enumerate([(mask_ref, mask_buf), (wq, wq_buf), (wk, wk_buf), (fields.at[lax.axis_index("segment") % 2 + 2], f_buf)])
    ]
    copies = [pltpu.make_async_copy(s, t, sems.at[i]) for i, (s, t) in enumerate(zip(big, held))]
    for c in early + copies:
        c.start()
    for c in early + copies[:4]:
        c.wait()
    n = o_ref.shape[0] - PAD
    kq_out[...] = queries_through_keys(lat_query, wq_buf, wk_buf)
    mask = feature_mask(rows_of(mask_buf, small), f_buf.shape[2], f_buf.shape[3])
    masked = flat(f_buf).astype(BF16) * mask
    o_ref[:n, :] = encode_unit(masked, score_ref, value_ref, kq_out, we, le, wv, wo)
    o_ref[n:, :] = jnp.zeros((PAD, o_ref.shape[1]), BF16)
    for c in copies[4:]:
        c.wait()


def hold_kernel(count, *refs):
    sems = refs[-1]
    copies = [pltpu.make_async_copy(refs[i], refs[count + i], sems.at[i]) for i in range(count)]
    for c in copies:
        c.start()
    for c in copies:
        c.wait()


def hold(arrays):
    count = len(arrays)
    return pl.pallas_call(
        functools.partial(hold_kernel, count),
        in_specs=[ANY] * count,
        out_specs=[VMEM] * count,
        out_shape=[pltpu.VMEM(a.shape, a.dtype) for a in arrays],
        scratch_shapes=[pltpu.SemaphoreType.DMA((count,))],
        compiler_params=params(12),
        name="hold",
    )(*[pltpu.with_memory_space_constraint(a, pltpu.HBM) for a in arrays])


def start(fields, valid_mask, lat_query, w_query, w_key, big):
    _, lats, cols, levels, feat = fields.shape
    latents, d = lat_query.shape
    cells = valid_mask.shape[-1]
    rows = lats * cols
    n = latents * rows
    hbm = [pltpu.with_memory_space_constraint(a, pltpu.HBM) for a in (fields, valid_mask)]
    more = [pltpu.with_memory_space_constraint(a, pltpu.HBM) for a in (w_query, w_key, *big)]
    out = pl.pallas_call(
        lambda *refs: start_kernel(len(big), *refs),
        in_specs=[ANY, ANY, VMEM] + [ANY] * (2 + len(big)),
        out_specs=[VMEM] * (2 + len(big)),
        out_shape=[
            jax.ShapeDtypeStruct((n + PAD, d), BF16),
            pltpu.VMEM((d, latents * HEADS), BF16),
        ] + [pltpu.VMEM(a.shape, a.dtype) for a in big],
        scratch_shapes=[
            pltpu.VMEM(fields.shape[1:], BF16),
            pltpu.VMEM(w_query.shape, BF16),
            pltpu.VMEM(w_key.shape, BF16),
            pltpu.VMEM(valid_mask.shape, jnp.int32),
            pltpu.VMEM((rows * levels, 128), F32),
            pltpu.VMEM((d // 128, rows * levels, 128), F32),
            pltpu.VMEM((rows, cells), F32),
            pltpu.SemaphoreType.DMA((len(big),)),
            pltpu.SemaphoreType.DMA((4,)),
        ],
        compiler_params=params(16),
        cost_estimate=pl.CostEstimate(flops=10**9, bytes_accessed=10**7, transcendentals=0),
        name="start",
    )(*hbm, lat_query, *more)
    return out[0], out[1], out[2:]


def own_slots(slot, before, after, rightward):
    held = (slot < before).astype(jnp.int32)
    wanted = (slot < after).astype(jnp.int32)
    wrapped = (after < before).astype(jnp.int32) if rightward else -(after > before).astype(jnp.int32)
    return wanted + wrapped == held


def gelu(x):
    cubic = SQRT_2_OVER_PI * 0.044715
    t = jnp.tanh(x * (x * x * jnp.asarray(cubic, x.dtype) + jnp.asarray(SQRT_2_OVER_PI, x.dtype)))
    half = x * jnp.asarray(0.5, x.dtype)
    return half * t + half


def attend(qkv_ref, mix_ref, lanes, d, width):
    window = qkv_ref.shape[0]
    per = lanes // width
    head_of = lax.broadcasted_iota(jnp.int32, (window, lanes), 1) // width
    row = lax.broadcasted_iota(jnp.int32, (1, lanes), 1) // width
    only = [(row == h).astype(F32).astype(BF16) for h in range(per)]
    ones = jnp.ones((window, lanes), BF16)
    for lo in range(0, d, lanes):
        q = qkv_ref[:, lo:lo + lanes]
        k = qkv_ref[:, d + lo:d + lo + lanes]
        v = qkv_ref[:, 2 * d + lo:2 * d + lo + lanes]
        scores = mm_t(jnp.concatenate([q * mask for mask in only], 0), k)
        probs = jnp.exp2((scores - jnp.max(scores, -1, keepdims=True)).astype(BF16))
        both = mm(probs, jnp.concatenate([v, ones], 1))
        num = both[:window, :lanes]
        den = both[:window, lanes:]
        for h in range(1, per):
            mine = head_of == h
            num = jnp.where(mine, both[h * window:(h + 1) * window, :lanes], num)
            den = jnp.where(mine, both[h * window:(h + 1) * window, lanes:], den)
        mix_ref[:, lo:lo + lanes] = (num / den).astype(BF16)
    return mix_ref[...]


def run_section(index, own_ref, nbr_ref, small, wqkv, wproj, wup, wdown, o_ref, qkv_ref, mix_ref):
    n, d = o_ref.shape[0] - PAD, o_ref.shape[1]
    width = d // HEADS
    window = qkv_ref.shape[0]
    passed = own_ref[n:, :].astype(F32)
    place = lax.broadcasted_iota(jnp.int32, (PAD, d), 0)
    shift = small[2:3, :].astype(F32)
    o_ref[n:, :] = jnp.where(place == index, shift, passed).astype(BF16)
    shift = shift[:, :1].astype(jnp.int32)
    before = jnp.sum(jnp.where(place == index - 1, passed, 0.0), 0, keepdims=True)[:, :1].astype(jnp.int32)
    slot = lax.broadcasted_iota(jnp.int32, (window, 1), 0) % WLON
    own = own_slots(slot, before, shift, index % 2 == 0)
    scale = width ** -0.5 * LOG2E

    @pl.loop(0, n // window)
    def _(w):
        at = pl.ds(pl.multiple_of(w * window, window), window)
        rolled = jnp.where(own, own_ref[at, :].astype(F32), nbr_ref[at, :].astype(F32))
        normed = norm(rolled, small[0:1, :]).astype(BF16)
        qkv_ref[:, :d] = (mm(normed, wqkv[0, :, :d]) * scale).astype(BF16)
        qkv_ref[:, d:] = mm(normed, wqkv[0, :, d:]).astype(BF16)
        acc = rolled + mm(attend(qkv_ref, mix_ref, 128, d, width), wproj[0])
        normed = norm(acc, small[1:2, :]).astype(BF16)
        step = 512
        for j in range(0, wup.shape[-1], step):
            hidden = gelu(mm(normed, wup[0, :, j:j + step]).astype(BF16))
            acc = acc + mm(hidden, wdown[0, j:j + step, :])
        o_ref[at, :] = acc.astype(BF16)


def tick_kernel(base, turn, own_ref, nbr_ref, *refs):
    given, received = refs[:5], refs[5:10]
    rest = refs[10:]
    mine = lax.axis_index("segment") % 2 == turn

    @pl.when(mine)
    def _():
        run_section(base + turn, own_ref, nbr_ref, *given, *rest)

    @pl.when(jnp.logical_not(mine))
    def _():
        run_section(base + turn, own_ref, nbr_ref, *received, *rest)


def tick(base, turn, own, nbr, given, received):
    rows, d = own.shape
    return pl.pallas_call(
        functools.partial(tick_kernel, base, turn),
        in_specs=[VMEM] * 12,
        out_specs=VMEM,
        out_shape=jax.ShapeDtypeStruct((rows, d), BF16),
        scratch_shapes=[pltpu.VMEM((WINDOW, 3 * d), BF16), pltpu.VMEM((WINDOW, d), BF16)],
        compiler_params=params(12),
        cost_estimate=pl.CostEstimate(flops=8 * 10**9, bytes_accessed=8 * 10**6, transcendentals=0),
        name="section",
    )(own, nbr, *given, *received)


def decode_kernel(state_ref, gain, w_ref, *refs):
    *arrived, o_ref = refs[:-1] if len(refs) == 3 else refs
    latents = w_ref.shape[0]
    n = state_ref.shape[0] - PAD
    rows = n // latents
    ours = lax.axis_index("segment") // 2 == 1

    @pl.when(ours)
    def _():
        normed = norm(state_ref[:n, :].astype(F32), gain[...])
        total = mm(normed[:rows].astype(BF16), w_ref[0])
        for i in range(1, latents):
            total = total + mm(normed[i * rows:(i + 1) * rows].astype(BF16), w_ref[i])
        passed = state_ref[n:, :o_ref.shape[1]].astype(F32)[:8]
        o_ref[...] = jnp.concatenate([total, passed], 0).astype(BF16)

    if arrived:
        @pl.when(jnp.logical_not(ours))
        def _():
            o_ref[...] = arrived[0][...]

        s = o_ref[...].astype(F32)[rows:]
        s = [s[i:i + 1, :] for i in range(4)]
        turns = jnp.zeros_like(s[0])
        for i in range(1, 4):
            if i % 2 == 0:
                turns = turns + (s[i] < s[i - 1]).astype(F32)
            else:
                turns = turns - (s[i] > s[i - 1]).astype(F32)
        refs[-1][0] = jnp.max(turns).astype(jnp.int32) + REACH


def decode(state, gain_dec, w_dec, *arrived):
    latents, _, outputs = w_dec.shape
    rows = (state.shape[0] - PAD) // latents
    more = len(arrived)
    return pl.pallas_call(
        decode_kernel,
        in_specs=[VMEM] * (3 + more),
        out_specs=[VMEM] + [SMEM] * more,
        out_shape=[jax.ShapeDtypeStruct((rows + 8, outputs), BF16)] + [jax.ShapeDtypeStruct((1,), jnp.int32)] * more,
        compiler_params=params(12),
        cost_estimate=pl.CostEstimate(flops=10**9, bytes_accessed=10**6, transcendentals=0),
        name="decode",
    )(state, gain_dec, w_dec, *arrived)


def home_kernel(*refs):
    same, before, mask_ref, targets, o_ref, sums_ref, x_ref, t_buf, t_ref, sem = refs
    copy = pltpu.make_async_copy(targets.at[:, :, lax.axis_index("segment")], t_buf, sem)
    copy.start()
    _, lats, cols, outs = o_ref.shape
    rows = lats * cols
    cells = mask_ref.shape[-1]
    shift = same[rows:, :].astype(F32)[3:4, :1].astype(jnp.int32)
    slot = lax.broadcasted_iota(jnp.int32, (rows, 1), 0) % WLON
    repeat = (
        lax.broadcasted_iota(jnp.int32, (cells, outs), 1) % cells
        == lax.broadcasted_iota(jnp.int32, (cells, outs), 0)
    ).astype(F32).astype(BF16)
    for i in range(lats):
        x_ref[i * cols:(i + 1) * cols, :cells] = mask_ref[i].astype(F32)
    weight = mm(x_ref[:, :cells].astype(BF16), repeat)
    guess = jnp.where(slot < shift, before[:rows, :].astype(F32), same[:rows, :].astype(F32))
    x_ref[...] = guess
    for i in range(lats):
        o_ref[0, i] = x_ref[i * cols:(i + 1) * cols, :].astype(BF16)
    copy.wait()
    for i in range(lats):
        x_ref[i * cols:(i + 1) * cols, :] = t_buf[i]
    truth = x_ref[...]
    misfit = guess - truth
    terms = (
        weight, weight * truth, weight * truth * truth, weight * guess, weight * guess * guess,
        weight * guess * truth, weight * misfit * misfit,
    )
    t_ref[...] = jnp.zeros(t_ref.shape, F32)
    for i, term in enumerate(terms):
        t_ref[i:i + 1, :] = jnp.sum(term, 0, keepdims=True)
    table = t_ref[...]
    n_var = outs // cells
    var_of = lax.broadcasted_iota(jnp.int32, table.shape, 1) // cells
    shape = (8, sums_ref.shape[-1])
    lane = lax.broadcasted_iota(jnp.int32, shape, 1)
    row = lax.broadcasted_iota(jnp.int32, shape, 0)
    flat = jnp.zeros(shape, F32)
    for v in range(n_var):
        part = jnp.sum(jnp.where(var_of == v, table, 0.0), -1, keepdims=True)
        flat = jnp.where(lane == row * n_var + v, part, flat)
    sums_ref[...] = jnp.broadcast_to(jnp.sum(flat, 0, keepdims=True), sums_ref.shape)


def at_home(cands, valid_mask, targets, devices):
    lats, cols, _, outs = targets.shape
    return pl.pallas_call(
        home_kernel,
        in_specs=[VMEM] * (len(cands) + 1) + [ANY],
        out_specs=[VMEM, VMEM],
        out_shape=[
            jax.ShapeDtypeStruct((1, lats, cols, outs), BF16),
            jax.ShapeDtypeStruct((devices, 128), F32),
        ],
        scratch_shapes=[
            pltpu.VMEM((lats * cols, outs), F32), pltpu.VMEM((lats, cols, outs), F32),
            pltpu.VMEM((8, outs), F32), pltpu.SemaphoreType.DMA,
        ],
        compiler_params=params(12),
        cost_estimate=pl.CostEstimate(flops=10**8, bytes_accessed=10**6, transcendentals=0),
        name="home",
    )(*cands, valid_mask, pltpu.with_memory_space_constraint(targets, pltpu.HBM))


def score_kernel(sums_ref, nse_ref, kge_ref, t_ref):
    n_var = nse_ref.shape[-1]
    total = jnp.sum(sums_ref[...], 0, keepdims=True)
    t_ref[...] = jnp.broadcast_to(total, t_ref.shape)
    t = [t_ref[:1, i * n_var:(i + 1) * n_var] for i in range(7)]
    number = jnp.maximum(t[0], 1.0)
    mean_obs = t[1] / number
    var_obs = t[2] / number - mean_obs * mean_obs
    mean_pred = t[3] / number
    var_pred = t[4] / number - mean_pred * mean_pred
    covariance = t[5] / number - mean_pred * mean_obs
    nse_ref[...] = 1.0 - t[6] / (number * var_obs)
    correlation = covariance / jnp.sqrt(var_pred * var_obs + EPSILON)
    spread_ratio = jnp.sqrt((var_pred + EPSILON) / var_obs)
    mean_ratio = mean_pred / mean_obs
    kge_ref[...] = 1.0 - jnp.sqrt(
        (correlation - 1.0) ** 2 + (spread_ratio - 1.0) ** 2 + (mean_ratio - 1.0) ** 2
    )


def scores(sums, n_var):
    return pl.pallas_call(
        score_kernel,
        in_specs=[VMEM],
        out_specs=[VMEM, VMEM],
        out_shape=[jax.ShapeDtypeStruct((1, n_var), F32)] * 2,
        scratch_shapes=[pltpu.VMEM((8, sums.shape[-1]), F32)],
        name="scores",
    )(sums)


def along(x, axis, distance):
    size = lax.axis_size(axis)
    return lax.ppermute(x, axis, [(i, (i + distance) % size) for i in range(size)])


def to_next_stage(x, turned):
    sections, tiles = lax.axis_size("segment"), lax.axis_size("tile")
    step = -1 if turned else 0
    route = [
        (k * tiles + t, (k + 2) % sections * tiles + (t + step) % tiles) for k in range(sections) for t in range(tiles)
    ]
    return lax.ppermute(x, ("segment", "tile"), route)


def from_other_core(x):
    return lax.ppermute(x, "segment", [(k, k ^ 1) for k in range(lax.axis_size("segment"))])


def way_home(turns, pred):
    return [pred if step == 0 else along(pred, "tile", step) for step in (turns, turns + 1)]


def local(
    fields, valid_mask, targets, w_embed, level_embed, lat_query, w_query, w_key, w_value, w_enc_out,
    gain_attn, w_qkv, w_proj, gain_mlp, w_up, w_down, gain_dec, w_dec, shifts,
):
    sections, tiles = lax.axis_size("segment"), lax.axis_size("tile")
    d = gain_attn.shape[1]
    fields = fields.transpose(0, 2, 3, 1, 4)
    targets = targets.transpose(1, 2, 0, 3)
    core = lax.axis_index("segment") % 2
    mask = jnp.tile(valid_mask.astype(BF16), (1, 1, fields.shape[-1] // valid_mask.shape[-1]))
    f_own = lax.dynamic_index_in_dim(fields, core, 0, keepdims=False) * mask[:, :, None, :]
    f_nbr = along(f_own, "tile", -1)
    plus, small = with_small(w_proj[0], gain_attn, gain_mlp, shifts)
    given = (small, w_qkv, w_proj, w_up, w_down)
    plus, *received = [from_other_core(a) for a in (plus, w_qkv, w_up, w_down)]
    received = hold(received)
    received = [plus[d:d + 3], received[0], plus[None, :d], *received[1:]]

    big = (w_embed, level_embed, w_value, w_enc_out, *given, w_dec)
    second, kq, held = start(fields, valid_mask, lat_query, w_query, w_key, big)
    enc = (kq, *held[:4])
    given = held[4:9]
    w_dec = held[9]
    gain_dec = gain_dec[None, :]

    second_nbr = along(second, "tile", -1)
    first = encode_rolled(f_own, f_nbr, given[0], received[0], enc)
    states = [first, second]
    nbrs = [first, second_nbr]
    for u in range(2):
        states[u] = tick(0, 0, states[u], nbrs[u], given, received)
        nbrs[u] = along(states[u], "tile", 1)
    for u in range(2):
        state = tick(0, 1, states[u], nbrs[u], given, received)
        states[u], nbrs[u] = to_next_stage(state, False), to_next_stage(state, True)
    for u in range(2):
        states[u] = tick(2, 0, states[u], nbrs[u], given, received)
        nbrs[u] = along(states[u], "tile", 1)
    for u in range(2):
        states[u] = tick(2, 1, states[u], nbrs[u], given, received)
        if u == 0:
            arrived = to_next_stage(decode(states[0], gain_dec, w_dec)[0], False)
    pred, turns = decode(states[1], gain_dec, w_dec, arrived)
    cands = lax.switch(turns[0], [functools.partial(way_home, t - REACH) for t in range(2 * REACH)], pred)
    predictions, sums = at_home(cands, valid_mask, targets, sections * tiles)
    sums = lax.all_to_all(sums, ("segment", "tile"), 0, 0, tiled=True)
    nse, kge = scores(sums, targets.shape[-1] // valid_mask.shape[-1])
    return predictions, nse[0], kge[0]


def encode_kernel(f_own, f_nbr, given, received, kq, we, le, wv, wo, o_ref, score_ref, value_ref):
    levels = f_own.shape[2]
    d = we.shape[1]
    shift = jnp.where(
        lax.axis_index("segment") % 2 == 0, given[2:3, :1].astype(F32), received[2:3, :1].astype(F32)
    ).astype(jnp.int32)
    own, nbr = flat(f_own), flat(f_nbr)
    slot = lax.broadcasted_iota(jnp.int32, (own.shape[0], 1), 0) // levels % WLON
    masked = jnp.where(slot < shift, nbr, own).astype(BF16)
    n = o_ref.shape[0] - PAD
    o_ref[:n, :] = encode_unit(masked, score_ref, value_ref, kq, we, le, wv, wo)
    o_ref[n:, :] = jnp.zeros((PAD, o_ref.shape[1]), BF16)


def encode_rolled(f_own, f_nbr, given, received, enc):
    lats, cols, levels, _ = f_own.shape
    d, n_q = enc[0].shape
    rows = lats * cols
    return pl.pallas_call(
        encode_kernel,
        in_specs=[VMEM] * (4 + len(enc)),
        out_specs=VMEM,
        out_shape=jax.ShapeDtypeStruct((n_q // HEADS * rows + PAD, d), BF16),
        scratch_shapes=[pltpu.VMEM((levels * rows, 128), F32), pltpu.VMEM((d // 128, levels * rows, 128), F32)],
        compiler_params=params(12),
        cost_estimate=pl.CostEstimate(flops=10**9, bytes_accessed=10**6, transcendentals=0),
        name="encode",
    )(f_own, f_nbr, given, received, *enc)


def solution(mesh):
    placed = (
        P(None, None, None, "tile", None),
        P(None, "tile", None),
        P(None, None, "tile", None),
        P(),
        P(),
        P(),
        P(),
        P(),
        P(),
        P(),
        P("segment", None),
        P("segment", None, None),
        P("segment", None, None),
        P("segment", None),
        P("segment", None, None),
        P("segment", None, None),
        P(),
        P(),
        P("segment"),
    )
    return jax.shard_map(
        local,
        mesh=mesh,
        in_specs=placed,
        out_specs=(P("segment", None, "tile", None), P(), P()),
        check_vma=False,
    )
```
